32 devices in a mesh: groups: 2 (over y), blk: 4 (over z), width: 4 (over x, core).
Axes of the slice: x: 2, y: 2, z: 4, core: 2. Of those that a mesh axis runs over, the one named last changes fastest.
Arguments:
- gate_pre: bfloat16 [448, 36864], P(('groups', 'width'), 'blk'), parts along dimension 0, may hold values from -6 to 6
- up_pre: bfloat16 [448, 36864], P(('groups', 'width'), 'blk'), parts along dimension 0, may hold values from -6 to 6
- down_weight: bfloat16 [36864, 9216], P('blk', 'width'), may hold values from -0.03125 to 0.03125
Outputs:
- mixed: bfloat16 [448, 9216], P(('groups', 'blk'), 'width'), parts along dimension 0
The draws below stay inside these ranges and needn't reach their ends.
There are 2 independent parts, one for each index of `groups`. The reference program is written for one: setup_inputs(seed, part) draws one part's arguments, and reference() takes and returns one part's arrays. A program takes and returns all parts, laid end to end along the dimension named above; an argument that names none is the same for every part. Nothing has to cross between parts.
All inputs are finite; a program needn't handle non-finite values.
Results may differ from the reference program's by a relative error of at most 0.009.
Values may be sent and summed in bfloat16 or wider, within the bound.
A program may use at most 128 MiB of HBM per device.

```python
import jax
import jax.numpy as jnp
from jax import lax

D = 9216
FF = 36864
TOKENS = 224
N_BLK = 4


def block_scale(key, extent, cuts, low, high):
    def one(axis_at, blocks):
        steps = jax.random.uniform(jax.random.fold_in(jax.random.fold_in(key, 6), axis_at), (blocks,), jnp.float32, low / len(cuts), high / len(cuts))
        return jnp.repeat(jnp.exp(steps), extent[axis_at] // blocks).reshape((-1,) + (1,) * (len(extent) - axis_at - 1))

    factor_of = one(*cuts[0])
    for cut in cuts[1:]:
        factor_of = factor_of * one(*cut)
    return factor_of


def scatter_about(own_key, shape, deviation, reach, shards=(), dtype=jnp.bfloat16):
    result = jax.random.normal(own_key, shape, jnp.float32) * deviation
    if len(shards) > 0:
        result = block_scale(own_key, shape, shards, -0.22, 0.18) * result
    return jnp.clip(result, min=-reach, max=reach).astype(dtype)


def setup_inputs(seed: int = 0, part: int = 0) -> dict:
    streams_of = jax.random.split(jax.random.key(seed), 4)
    part_keys = jax.random.split(jax.random.fold_in(streams_of[3], part), 4)
    return {
        "gate_pre": scatter_about(part_keys[0], (TOKENS, FF), 1.0, 6.0, ((0, 4), (1, 4))),
        "up_pre": scatter_about(part_keys[1], (TOKENS, FF), 1.0, 6.0, ((0, 4), (1, 4))),
        "down_weight": scatter_about(streams_of[2], (FF, D), FF ** -0.5, 0.03125, ((0, 4), (1, 4))),
    }


def reference(gate_pre, up_pre, down_weight):
    part_f = FF // N_BLK
    gate = gate_pre.astype(jnp.float32)
    up = up_pre.astype(jnp.float32)
    hidden = (jax.nn.silu(gate) * up).astype(jnp.bfloat16)
    hs = hidden.reshape(TOKENS, N_BLK, part_f).transpose(1, 0, 2)
    ds = down_weight.reshape(N_BLK, part_f, D)

    def down_step(carry, block):
        h_block, d_block = block
        term = jnp.dot(h_block, d_block, preferred_element_type=jnp.float32).astype(jnp.bfloat16)
        term = lax.optimization_barrier(term)
        return carry + term.astype(jnp.float32), None

    total, _ = lax.scan(down_step, jnp.zeros((TOKENS, D), jnp.float32), (hs, ds))
    return total.astype(jnp.bfloat16)
```

```python
import functools

import jax
import jax.numpy as jnp
from jax import lax
from jax.experimental import pallas as pl
from jax.experimental.pallas import tpu as pltpu
from jax.sharding import PartitionSpec as P

PIECES = 3
AHEAD = 2
HOP = 3
GAP = 3


def kernel(
    B, W, gate, up, weight, out,
    gate_v, up_v, w_v, hid_a, hid_b, acc_a, acc_b, tmp, send_buf, from_below, from_above,
    in_sem, w_sem, sib_send, sib_recv, x_send, x_recv, fwd_send, fwd_recv, rs_send, rs_below, rs_above,
):
    X = W // 2
    C, R, Kc = gate_v.shape
    q = B // W
    r = R // q
    Np = acc_a.shape[2]
    nA, nB = X + 1, X - 1
    z = lax.axis_index("blk")
    width = lax.axis_index("width")
    p, k = width // 2, width % 2
    sibling = {"width": p * 2 + 1 - k}
    first = (p * 2) // X

    def load(c):
        cols = pl.ds(pl.multiple_of(c * Kc, 128), Kc)
        return (
            pltpu.make_async_copy(gate.at[:, cols], gate_v.at[c], in_sem.at[0, c]),
            pltpu.make_async_copy(up.at[:, cols], up_v.at[c], in_sem.at[1, c]),
        )

    def load_weight(c):
        rows = pl.ds(pl.multiple_of(c * Kc, 128), Kc)
        return pltpu.make_async_copy(weight.at[rows, :], w_v.at[c], w_sem.at[c])

    def to_sibling(c):
        return pltpu.make_async_remote_copy(
            hid_a.at[c, k], hid_a.at[c, k], sib_send.at[c], sib_recv.at[c],
            device_id=sibling, device_id_type=pl.DeviceIdType.MESH,
        )

    def from_sibling(c):
        return pltpu.make_async_remote_copy(
            hid_a.at[c, 1 - k], hid_a.at[c, 1 - k], sib_send.at[c], sib_recv.at[c],
            device_id=sibling, device_id_type=pl.DeviceIdType.MESH,
        )

    def across(phase, o, c):
        peer = lax.rem(p + o, X) * 2 + k
        src = hid_a.at[c, first] if phase == 0 else hid_a.at[c, 1 - first]
        dst = hid_a.at[c, 1 + o] if phase == 0 else hid_b.at[c, o - 1]
        return pltpu.make_async_remote_copy(
            src, dst, x_send.at[phase, o - 1, c], x_recv.at[phase, o - 1, c],
            device_id={"width": peer}, device_id_type=pl.DeviceIdType.MESH,
        )

    def forward(phase, o, c):
        ref = hid_a.at[c, 1 + o] if phase == 0 else hid_b.at[c, o - 1]
        return pltpu.make_async_remote_copy(
            ref, ref, fwd_send.at[phase, o - 1, c], fwd_recv.at[phase, o - 1, c],
            device_id=sibling, device_id_type=pl.DeviceIdType.MESH,
        )

    def mine(c):
        return lax.rem(c, 2) == k

    def send_across(phase, c):
        for o in range(1, X):
            across(phase, o, c).start()

    def service(phase, c):
        @pl.when(mine(c))
        def _():
            for o in range(1, X):
                across(phase, o, c).wait_recv()
                forward(phase, o, c).start()

    def arrived(phase, c):
        @pl.when(jnp.logical_not(mine(c)))
        def _():
            for o in range(1, X):
                forward(phase, o, c).wait_recv()

    def loop(n, body):
        lax.fori_loop(0, n, lambda i, _: (body(i), 0)[1], 0)

    def start_loads(c):
        a, b = load(c)
        a.start()
        b.start()

    loop(C, start_loads)
    loop(C, lambda c: load_weight(c).start())

    barrier = pltpu.get_barrier_semaphore()

    def greet(device):
        pl.semaphore_signal(barrier, inc=1, device_id=device, device_id_type=pl.DeviceIdType.MESH)

    greet(sibling)
    for o in range(1, X):
        greet({"width": lax.rem(p + o, X) * 2 + k})
    pl.when(z > 0)(lambda: greet({"blk": z - 1}))
    pl.when(z < B - 1)(lambda: greet({"blk": z + 1}))
    pl.semaphore_wait(barrier, X + jnp.minimum(z, 1) + jnp.minimum(B - 1 - z, 1))

    def activate(c):
        a, b = load(c)
        a.wait()
        b.wait()
        v = gate_v[c].astype(jnp.float32)
        h = v / (1.0 + jnp.exp(-v)) * up_v[c].astype(jnp.float32)
        hid_a[c, k] = h.astype(jnp.bfloat16)
        pl.when(jnp.logical_and(mine(c), first == k))(lambda: send_across(0, c))
        to_sibling(c).start()

    loop(C, activate)

    def exchange(c):
        from_sibling(c).wait_recv()
        pl.when(jnp.logical_and(mine(c), first != k))(lambda: send_across(0, c))

    loop(C, exchange)

    def multiply(hid, acc, c, pieces):
        n_slots = hid.shape[1]
        lhs = hid[c].reshape(n_slots * R, Kc)
        for n in pieces:
            acc[n] += jnp.dot(
                lhs, w_v[c, :, n * Np : (n + 1) * Np], preferred_element_type=jnp.float32
            )

    acc_a[...] = jnp.zeros_like(acc_a)
    acc_b[...] = jnp.zeros_like(acc_b)
    ahead = min(AHEAD, C)
    for c in range(ahead):
        service(0, c)

    def step_a(c):
        pl.when(c + ahead < C)(lambda: service(0, c + ahead))
        pl.when(mine(c))(lambda: send_across(1, c))
        load_weight(c).wait()
        arrived(0, c)
        multiply(hid_a, acc_a, c, range(PIECES))

    loop(C, step_a)

    def hop(acc, idx, step, j, n):
        rows = pl.ds(pl.multiple_of(idx * r, 8), r)
        below = pltpu.make_async_remote_copy(
            send_buf.at[step], from_below.at[step], rs_send.at[step], rs_below.at[step],
            device_id={"blk": jnp.minimum(z + 1, B - 1)}, device_id_type=pl.DeviceIdType.MESH,
        )
        above = pltpu.make_async_remote_copy(
            send_buf.at[step], from_above.at[step], rs_send.at[step], rs_above.at[step],
            device_id={"blk": jnp.maximum(z - 1, 0)}, device_id_type=pl.DeviceIdType.MESH,
        )
        tmp[...] = acc[n, rows, :]

        @pl.when(jnp.logical_and(z <= j, z > 0))
        def _():
            below.wait_recv()
            tmp[...] += from_below[step].astype(jnp.float32)

        @pl.when(jnp.logical_and(z >= j, z < B - 1))
        def _():
            above.wait_recv()
            tmp[...] += from_above[step].astype(jnp.float32)

        @pl.when(z != j)
        def _():
            send_buf[step] = tmp[...].astype(jnp.bfloat16)

        pl.when(z < j)(lambda: below.start())
        pl.when(z > j)(lambda: above.start())

        @pl.when(z == j)
        def _():
            out[:, pl.ds(pl.multiple_of(n * Np, 128), Np)] = tmp[...].astype(jnp.bfloat16)

    def slab_of(slot):
        o = jnp.where(slot < nA, slot - 1, slot - nA + 1)
        chip = lax.rem(p - o + 2 * X, X)
        lead = (chip * 2) // X
        remote = chip * 2 + jnp.where(slot < nA, lead, 1 - lead)
        return jnp.where(slot < 2, p * 2 + slot, remote)

    def distance(j):
        return jnp.where(z < j, z, jnp.where(z > j, B - 1 - z, jnp.maximum(z, B - 1 - z)))

    def reduce_a(t):
        def one(idx):
            j = slab_of(idx // q) * q + lax.rem(idx, q)
            rest = t - distance(j) * HOP
            n = rest // GAP

            @pl.when(jnp.logical_and(rest >= 0, jnp.logical_and(rest == n * GAP, n < PIECES)))
            def _():
                hop(acc_a, idx, idx * PIECES + n, j, n)

        loop(nA * q, one)

    def reduce_b(n, ends):
        def one(idx):
            j = slab_of(nA + idx // q) * q + lax.rem(idx, q)
            end = jnp.logical_or(
                jnp.logical_and(z < j, z == 0), jnp.logical_and(z > j, z == B - 1)
            )

            @pl.when(end == ends)
            def _():
                hop(acc_b, idx, (nA * q + idx) * PIECES + n, j, n)

        loop(nB * q, one)

    for c in range(ahead):
        service(1, c)

    def step_b(c):
        pl.when(c + ahead < C)(lambda: service(1, c + ahead))
        reduce_a(c)
        arrived(1, c)
        multiply(hid_b, acc_b, c, range(PIECES))

    loop(C - 1, step_b)
    arrived(1, C - 1)
    for n in range(PIECES):
        multiply(hid_b, acc_b, C - 1, [n])
        reduce_b(n, True)
    last = (B - 1) * HOP + (PIECES - 1) * GAP
    loop(max(last + 1 - (C - 1), 0), lambda t: reduce_a(t + C - 1))
    loop(PIECES, lambda n: reduce_b(n, False))

    def finish(c):
        to_sibling(c).wait_send()

        @pl.when(mine(c))
        def _():
            for phase in range(2):
                for o in range(1, X):
                    across(phase, o, c).wait_send()
                    forward(phase, o, c).wait_send()

    loop(C, finish)

    def finish_sum(step):
        slot = step // (PIECES * q)
        j = slab_of(slot) * q + lax.rem(step // PIECES, q)

        @pl.when(z != j)
        def _():
            pltpu.make_async_remote_copy(
                send_buf.at[step], from_below.at[step], rs_send.at[step], rs_below.at[step],
                device_id={"blk": jnp.where(z < j, z + 1, z - 1)},
                device_id_type=pl.DeviceIdType.MESH,
            ).wait_send()

    loop(W * q * PIECES, finish_sum)


def per_device(B, W, gate_pre, up_pre, down_weight):
    R, K = gate_pre.shape
    N = down_weight.shape[1]
    X = W // 2
    Kc = next(s for s in (768, 384, 256, 128) if K % s == 0)
    C = K // Kc
    r = R * W // B
    Np = N // PIECES
    steps = B * PIECES
    bf16, f32 = jnp.bfloat16, jnp.float32
    dma = pltpu.SemaphoreType.DMA
    return pl.pallas_call(
        functools.partial(kernel, B, W),
        out_shape=jax.ShapeDtypeStruct((r, N), bf16),
        in_specs=[pl.BlockSpec(memory_space=pl.ANY)] * 3,
        out_specs=pl.BlockSpec(memory_space=pltpu.VMEM),
        scratch_shapes=[
            pltpu.VMEM((C, R, Kc), bf16),
            pltpu.VMEM((C, R, Kc), bf16),
            pltpu.VMEM((C, Kc, N), bf16),
            pltpu.VMEM((C, X + 1, R, Kc), bf16),
            pltpu.VMEM((C, X - 1, R, Kc), bf16),
            pltpu.VMEM((PIECES, (X + 1) * R, Np), f32),
            pltpu.VMEM((PIECES, (X - 1) * R, Np), f32),
            pltpu.VMEM((r, Np), f32),
            pltpu.VMEM((steps, r, Np), bf16),
            pltpu.VMEM((steps, r, Np), bf16),
            pltpu.VMEM((steps, r, Np), bf16),
            dma((2, C)),
            dma((C,)),
            dma((C,)),
            dma((C,)),
            dma((2, X - 1, C)),
            dma((2, X - 1, C)),
            dma((2, X - 1, C)),
            dma((2, X - 1, C)),
            dma((steps,)),
            dma((steps,)),
            dma((steps,)),
        ],
        compiler_params=pltpu.CompilerParams(
            collective_id=0, has_side_effects=True, vmem_limit_bytes=62 * 1024 * 1024
        ),
    )(gate_pre, up_pre, down_weight)


def solution(mesh):
    return jax.shard_map(
        functools.partial(per_device, mesh.shape["blk"], mesh.shape["width"]),
        mesh=mesh,
        in_specs=(P(("groups", "width"), "blk"), P(("groups", "width"), "blk"), P("blk", "width")),
        out_specs=P(("groups", "blk"), "width"),
        check_vma=False,
    )
```

```python
import functools

import jax
import jax.numpy as jnp
from jax import lax
from jax.experimental import pallas as pl
from jax.experimental.pallas import tpu as pltpu
from jax.sharding import PartitionSpec as P

PIECES = 3
AHEAD = 1
HOP = 2
GAP = 1


def kernel(
    B, W, gate, up, weight, out,
    gate_v, up_v, w_v, hid_a, hid_b, acc_a, acc_b, tmp, send_buf, from_below, from_above,
    in_sem, w_sem, sib_send, sib_recv, x_send, x_recv, fwd_send, fwd_recv, rs_send, rs_below, rs_above,
):
    X = W // 2
    C, R, Kc = gate_v.shape
    q = B // W
    r = R // q
    Np = acc_a.shape[2]
    nA, nB = X + 1, X - 1
    z = lax.axis_index("blk")
    width = lax.axis_index("width")
    p, k = width // 2, width % 2
    sibling = {"width": p * 2 + 1 - k}
    first = (p * 2) // X

    def load(c):
        cols = pl.ds(pl.multiple_of(c * Kc, 128), Kc)
        return (
            pltpu.make_async_copy(gate.at[:, cols], gate_v.at[c], in_sem.at[0, c]),
            pltpu.make_async_copy(up.at[:, cols], up_v.at[c], in_sem.at[1, c]),
        )

    def load_weight(c):
        rows = pl.ds(pl.multiple_of(c * Kc, 128), Kc)
        return pltpu.make_async_copy(weight.at[rows, :], w_v.at[c], w_sem.at[c])

    def to_sibling(c):
        return pltpu.make_async_remote_copy(
            hid_a.at[c, k], hid_a.at[c, k], sib_send.at[c], sib_recv.at[c],
            device_id=sibling, device_id_type=pl.DeviceIdType.MESH,
        )

    def from_sibling(c):
        return pltpu.make_async_remote_copy(
            hid_a.at[c, 1 - k], hid_a.at[c, 1 - k], sib_send.at[c], sib_recv.at[c],
            device_id=sibling, device_id_type=pl.DeviceIdType.MESH,
        )

    def across(phase, o, c):
        peer = lax.rem(p + o, X) * 2 + k
        src = hid_a.at[c, first] if phase == 0 else hid_a.at[c, 1 - first]
        dst = hid_a.at[c, 1 + o] if phase == 0 else hid_b.at[c, o - 1]
        return pltpu.make_async_remote_copy(
            src, dst, x_send.at[phase, o - 1, c], x_recv.at[phase, o - 1, c],
            device_id={"width": peer}, device_id_type=pl.DeviceIdType.MESH,
        )

    def forward(phase, o, c):
        ref = hid_a.at[c, 1 + o] if phase == 0 else hid_b.at[c, o - 1]
        return pltpu.make_async_remote_copy(
            ref, ref, fwd_send.at[phase, o - 1, c], fwd_recv.at[phase, o - 1, c],
            device_id=sibling, device_id_type=pl.DeviceIdType.MESH,
        )

    def mine(c):
        return lax.rem(c, 2) == k

    def send_across(phase, c):
        for o in range(1, X):
            across(phase, o, c).start()

    def service(phase, c):
        @pl.when(mine(c))
        def _():
            for o in range(1, X):
                across(phase, o, c).wait_recv()
                forward(phase, o, c).start()

    def arrived(phase, c):
        @pl.when(jnp.logical_not(mine(c)))
        def _():
            for o in range(1, X):
                forward(phase, o, c).wait_recv()

    def loop(n, body):
        lax.fori_loop(0, n, lambda i, _: (body(i), 0)[1], 0)

    def start_loads(c):
        a, b = load(c)
        a.start()
        b.start()

    loop(C, start_loads)
    loop(C, lambda c: load_weight(c).start())

    barrier = pltpu.get_barrier_semaphore()

    def greet(device):
        pl.semaphore_signal(barrier, inc=1, device_id=device, device_id_type=pl.DeviceIdType.MESH)

    greet(sibling)
    for o in range(1, X):
        greet({"width": lax.rem(p + o, X) * 2 + k})
    pl.when(z > 0)(lambda: greet({"blk": z - 1}))
    pl.when(z < B - 1)(lambda: greet({"blk": z + 1}))
    acc_a[...] = jnp.zeros_like(acc_a)
    acc_b[...] = jnp.zeros_like(acc_b)
    pl.semaphore_wait(barrier, X + jnp.minimum(z, 1) + jnp.minimum(B - 1 - z, 1))

    def activate(c):
        a, b = load(c)
        a.wait()
        b.wait()
        v = gate_v[c].astype(jnp.float32)
        h = v / (1.0 + jnp.exp(-v)) * up_v[c].astype(jnp.float32)
        hid_a[c, k] = h.astype(jnp.bfloat16)
        pl.when(jnp.logical_and(mine(c), first == k))(lambda: send_across(0, c))
        to_sibling(c).start()

    loop(C, activate)

    def exchange(c):
        from_sibling(c).wait_recv()
        pl.when(jnp.logical_and(mine(c), first != k))(lambda: send_across(0, c))

    loop(C, exchange)

    def multiply(hid, acc, c, pieces):
        n_slots = hid.shape[1]
        lhs = hid[c].reshape(n_slots * R, Kc)
        for n in pieces:
            acc[n] += jnp.dot(
                lhs, w_v[c, :, n * Np : (n + 1) * Np], preferred_element_type=jnp.float32
            )

    ahead = min(AHEAD, C)
    for c in range(ahead):
        service(0, c)

    def step_a(c):
        pl.when(c + ahead < C)(lambda: service(0, c + ahead))
        pl.when(mine(c))(lambda: send_across(1, c))
        load_weight(c).wait()
        arrived(0, c)
        multiply(hid_a, acc_a, c, range(PIECES))

    loop(C, step_a)

    def hop(acc, idx, step, j, n):
        rows = pl.ds(pl.multiple_of(idx * r, 8), r)
        below = pltpu.make_async_remote_copy(
            send_buf.at[step], from_below.at[step], rs_send.at[step], rs_below.at[step],
            device_id={"blk": jnp.minimum(z + 1, B - 1)}, device_id_type=pl.DeviceIdType.MESH,
        )
        above = pltpu.make_async_remote_copy(
            send_buf.at[step], from_above.at[step], rs_send.at[step], rs_above.at[step],
            device_id={"blk": jnp.maximum(z - 1, 0)}, device_id_type=pl.DeviceIdType.MESH,
        )
        tmp[...] = acc[n, rows, :]

        @pl.when(jnp.logical_and(z <= j, z > 0))
        def _():
            below.wait_recv()
            tmp[...] += from_below[step].astype(jnp.float32)

        @pl.when(jnp.logical_and(z >= j, z < B - 1))
        def _():
            above.wait_recv()
            tmp[...] += from_above[step].astype(jnp.float32)

        @pl.when(z != j)
        def _():
            send_buf[step] = tmp[...].astype(jnp.bfloat16)

        pl.when(z < j)(lambda: below.start())
        pl.when(z > j)(lambda: above.start())

        @pl.when(z == j)
        def _():
            out[:, pl.ds(pl.multiple_of(n * Np, 128), Np)] = tmp[...].astype(jnp.bfloat16)

    def slab_of(slot):
        o = jnp.where(slot < nA, slot - 1, slot - nA + 1)
        chip = lax.rem(p - o + 2 * X, X)
        lead = (chip * 2) // X
        remote = chip * 2 + jnp.where(slot < nA, lead, 1 - lead)
        return jnp.where(slot < 2, p * 2 + slot, remote)

    def distance(j):
        return jnp.where(z < j, z, jnp.where(z > j, B - 1 - z, jnp.maximum(z, B - 1 - z)))

    def reduce_a(t):
        def one(idx):
            j = slab_of(idx // q) * q + lax.rem(idx, q)
            rest = t - distance(j) * HOP
            n = rest // GAP

            @pl.when(jnp.logical_and(rest >= 0, jnp.logical_and(rest == n * GAP, n < PIECES)))
            def _():
                hop(acc_a, idx, idx * PIECES + n, j, n)

        loop(nA * q, one)

    def reduce_b(n, ends):
        def one(idx):
            j = slab_of(nA + idx // q) * q + lax.rem(idx, q)
            end = jnp.logical_or(
                jnp.logical_and(z < j, z == 0), jnp.logical_and(z > j, z == B - 1)
            )

            @pl.when(end == ends)
            def _():
                hop(acc_b, idx, (nA * q + idx) * PIECES + n, j, n)

        loop(nB * q, one)

    for c in range(ahead):
        service(1, c)

    def step_b(c):
        pl.when(c + ahead < C)(lambda: service(1, c + ahead))
        reduce_a(c)
        arrived(1, c)
        multiply(hid_b, acc_b, c, range(PIECES))

    loop(C - 1, step_b)
    arrived(1, C - 1)
    for n in range(PIECES):
        multiply(hid_b, acc_b, C - 1, [n])
        reduce_b(n, True)
    last = (B - 1) * HOP + (PIECES - 1) * GAP
    loop(max(last + 1 - (C - 1), 0), lambda t: reduce_a(t + C - 1))
    loop(PIECES, lambda n: reduce_b(n, False))

    def finish(c):
        to_sibling(c).wait_send()

        @pl.when(mine(c))
        def _():
            for phase in range(2):
                for o in range(1, X):
                    across(phase, o, c).wait_send()
                    forward(phase, o, c).wait_send()

    loop(C, finish)

    def finish_sum(step):
        slot = step // (PIECES * q)
        j = slab_of(slot) * q + lax.rem(step // PIECES, q)

        @pl.when(z != j)
        def _():
            pltpu.make_async_remote_copy(
                send_buf.at[step], from_below.at[step], rs_send.at[step], rs_below.at[step],
                device_id={"blk": jnp.where(z < j, z + 1, z - 1)},
                device_id_type=pl.DeviceIdType.MESH,
            ).wait_send()

    loop(W * q * PIECES, finish_sum)


def per_device(B, W, gate_pre, up_pre, down_weight):
    R, K = gate_pre.shape
    N = down_weight.shape[1]
    X = W // 2
    Kc = next(s for s in (1536, 384, 256, 128) if K % s == 0)
    C = K // Kc
    r = R * W // B
    Np = N // PIECES
    steps = B * PIECES
    bf16, f32 = jnp.bfloat16, jnp.float32
    dma = pltpu.SemaphoreType.DMA
    return pl.pallas_call(
        functools.partial(kernel, B, W),
        out_shape=jax.ShapeDtypeStruct((r, N), bf16),
        in_specs=[pl.BlockSpec(memory_space=pl.ANY)] * 3,
        out_specs=pl.BlockSpec(memory_space=pltpu.VMEM),
        scratch_shapes=[
            pltpu.VMEM((C, R, Kc), bf16),
            pltpu.VMEM((C, R, Kc), bf16),
            pltpu.VMEM((C, Kc, N), bf16),
            pltpu.VMEM((C, X + 1, R, Kc), bf16),
            pltpu.VMEM((C, X - 1, R, Kc), bf16),
            pltpu.VMEM((PIECES, (X + 1) * R, Np), f32),
            pltpu.VMEM((PIECES, (X - 1) * R, Np), f32),
            pltpu.VMEM((r, Np), f32),
            pltpu.VMEM((steps, r, Np), bf16),
            pltpu.VMEM((steps, r, Np), bf16),
            pltpu.VMEM((steps, r, Np), bf16),
            dma((2, C)),
            dma((C,)),
            dma((C,)),
            dma((C,)),
            dma((2, X - 1, C)),
            dma((2, X - 1, C)),
            dma((2, X - 1, C)),
            dma((2, X - 1, C)),
            dma((steps,)),
            dma((steps,)),
            dma((steps,)),
        ],
        compiler_params=pltpu.CompilerParams(
            collective_id=0, has_side_effects=True, vmem_limit_bytes=62 * 1024 * 1024
        ),
    )(gate_pre, up_pre, down_weight)


def solution(mesh):
    return jax.shard_map(
        functools.partial(per_device, mesh.shape["blk"], mesh.shape["width"]),
        mesh=mesh,
        in_specs=(P(("groups", "width"), "blk"), P(("groups", "width"), "blk"), P("blk", "width")),
        out_specs=P(("groups", "blk"), "width"),
        check_vma=False,
    )
```
